32 devices in a mesh: branch: 4 (over y, x), leaf: 8 (over z, core).
Axes of the slice: x: 2, y: 2, z: 4, core: 2. Of those that a mesh axis runs over, the one named last changes fastest.
Arguments:
- charges: bfloat16 [256, 16, 128], P(('branch', 'leaf')), may hold values from -6 to 6
- basis: bfloat16 [256, 128, 128], P(('branch', 'leaf')), may hold values from -0.5 to 0.5
- transfer0: bfloat16 [256, 128, 128], P(('branch', 'leaf')), may hold values from -0.5 to 0.5
- transfer1: bfloat16 [128, 128, 128], P(('branch', 'leaf')), may hold values from -0.5 to 0.5
- transfer2: bfloat16 [64, 128, 128], P(('branch', 'leaf')), may hold values from -0.5 to 0.5
- couple0: bfloat16 [256, 8, 128, 128], P(('branch', 'leaf')), may hold values from -0.1875 to 0.1875
- couple1: bfloat16 [128, 8, 128, 128], P(('branch', 'leaf')), may hold values from -0.1875 to 0.1875
- couple2: bfloat16 [64, 8, 128, 128], P(('branch', 'leaf')), may hold values from -0.1875 to 0.1875
- couple_top: bfloat16 [32, 8, 128, 128], P(('branch', 'leaf')), may hold values from -0.1875 to 0.1875
- list0: int32 [256, 8], P(('branch', 'leaf')), may hold values from 0 to 63, as said below
- list1: int32 [128, 8], P(('branch', 'leaf')), may hold values from 0 to 31, as said below
- list2: int32 [64, 8], P(('branch', 'leaf')), may hold values from 0 to 15, as said below
- mask0: int32 [256, 8], P(('branch', 'leaf')), may hold values from 0 to 1, as said below
- mask1: int32 [128, 8], P(('branch', 'leaf')), may hold values from 0 to 1, as said below
- mask2: int32 [64, 8], P(('branch', 'leaf')), may hold values from 0 to 1, as said below
- top_list: int32 [32, 8], P(('branch', 'leaf')), may hold values from 0 to 31
- top_mask: int32 [32, 8], P(('branch', 'leaf')), may hold values 0 or 1
- near_tiles: bfloat16 [256, 8, 128, 128], P(('branch', 'leaf')), may hold values from -0.1875 to 0.1875
- near_list: int32 [256, 8], P(('branch', 'leaf')), may hold values from 0 to 63, as said below
- near_mask: int32 [256, 8], P(('branch', 'leaf')), may hold values from 0 to 1, as said below
Outputs:
- potential: float32 [256, 16, 128], P(('branch', 'leaf'))
The draws below stay inside these ranges and needn't reach their ends.
Inputs may be any that keep to these rules, and one draw needn't show every extreme that they name: `list0`: each entry names a leaf of the row's branch group owned by the row's device or one of the two devices beside it along leaf. `list1`: each entry names a level one cluster of the row's branch group owned by the row's device or one of the two devices beside it along leaf. `list2`: each entry names a level two cluster of the row's branch group owned by the row's device or one of the two devices beside it along leaf. `near_list`: each entry names a leaf of the row's branch group owned by the row's device or one of the two devices beside it along leaf. `mask0`: 1 marks a live entry. `mask1`: 1 marks a live entry. `mask2`: 1 marks a live entry. `near_mask`: 1 marks a live entry.
All inputs are finite; a program needn't handle non-finite values. No bound on the sum of `top_mask` on one device may be relied on, other than what follows from the above.
Results may differ from the reference program's by a relative error of at most 0.015.
Values may be sent and summed in bfloat16 or wider, within the bound.
A program may use at most 64 MiB of HBM per device.

```python
import jax
import jax.numpy as jnp
from jax import lax

LEAF = 128
RANK = 128
NRHS = 16
CL_DEV = 8
KC = 8
KT = 8
NEAR = 8
LEAVES = 256
LEVEL1 = 128
LEVEL2 = 64
TOPS = 32
N_BRANCH = 4
N_LEAF = 8


def pick_blocks(key, count, width, salt):
    key = jax.random.fold_in(key, salt)
    rows = N_BRANCH * N_LEAF * count
    spot = jnp.arange(rows, dtype=jnp.int32) % (N_LEAF * count)
    first = spot // count * count - count
    offset = jax.random.randint(jax.random.fold_in(key, 1), (rows, width), 0, 3 * count, dtype=jnp.int32)
    target = first[:, None] + offset
    inside = (target >= 0) & (target < N_LEAF * count)
    chosen = jax.random.randint(jax.random.fold_in(key, 2), (rows, width), 0, 4, dtype=jnp.int32) < 3
    links = jnp.clip(target, 0, N_LEAF * count - 1).astype(jnp.int32)
    return (links, (inside & chosen).astype(jnp.int32))


def draw_list0(key, part):
    return pick_blocks(key, CL_DEV, KC, 11)[0]


def draw_mask0(key, part):
    return pick_blocks(key, CL_DEV, KC, 11)[1]


def draw_list1(key, part):
    return pick_blocks(key, CL_DEV // 2, KC, 12)[0]


def draw_mask1(key, part):
    return pick_blocks(key, CL_DEV // 2, KC, 12)[1]


def draw_list2(key, part):
    return pick_blocks(key, CL_DEV // 4, KC, 13)[0]


def draw_mask2(key, part):
    return pick_blocks(key, CL_DEV // 4, KC, 13)[1]


def draw_near_list(key, part):
    return pick_blocks(key, CL_DEV, NEAR, 14)[0]


def draw_near_mask(key, part):
    return pick_blocks(key, CL_DEV, NEAR, 14)[1]


def plant(result, key, least, high):
    longest = result.shape.index(max(result.shape))
    spots = []
    for shift in (0, 1):
        where = [jax.random.randint(jax.random.fold_in(key, axis), (), 0, length) for axis, length in enumerate(result.shape)]
        where[longest] = (where[longest] + shift) % result.shape[longest]
        spots.append(tuple(where))
    return result.at[spots[0]].set(least).at[spots[1]].set(high)


def level_of(key, dims, shards, least, high):
    factor_of = 1.0
    for dim, blocks in shards:
        steps = jax.random.uniform(jax.random.fold_in(jax.random.fold_in(key, 6), dim), (blocks,), jnp.float32, least / len(shards), high / len(shards))
        factor_of = factor_of * jnp.repeat(jnp.exp(steps), dims[dim] // blocks).reshape((-1,) + (1,) * (len(dims) - 1 - dim))
    return factor_of


def scatter_about(rng, shape, scale, most, pieces=(), kind=jnp.bfloat16):
    entries = jax.random.normal(rng, shape, jnp.float32) * scale
    if len(pieces) > 0:
        entries = level_of(rng, shape, pieces, -0.22, 0.18) * entries
    return jnp.clip(entries, min=-most, max=most).astype(kind)


def setup_inputs(seed: int = 0) -> dict:
    splits = jax.random.split(jax.random.key(seed), 21)
    return {
        "charges": scatter_about(splits[0], (LEAVES, NRHS, LEAF), 1.0, 6.0, ((0, 32),)),
        "basis": scatter_about(splits[1], (LEAVES, LEAF, RANK), LEAF ** -0.5, 0.5, ((0, 32),)),
        "transfer0": scatter_about(splits[2], (LEAVES, RANK, RANK), RANK ** -0.5, 0.5, ((0, 32),)),
        "transfer1": scatter_about(splits[3], (LEVEL1, RANK, RANK), RANK ** -0.5, 0.5, ((0, 32),)),
        "transfer2": scatter_about(splits[4], (LEVEL2, RANK, RANK), RANK ** -0.5, 0.5, ((0, 32),)),
        "couple0": scatter_about(splits[5], (LEAVES, KC, RANK, RANK), (RANK * KC) ** -0.5, 0.1875, ((0, 32),)),
        "couple1": scatter_about(splits[6], (LEVEL1, KC, RANK, RANK), (RANK * KC) ** -0.5, 0.1875, ((0, 32),)),
        "couple2": scatter_about(splits[7], (LEVEL2, KC, RANK, RANK), (RANK * KC) ** -0.5, 0.1875, ((0, 32),)),
        "couple_top": scatter_about(splits[8], (TOPS, KT, RANK, RANK), (RANK * KT) ** -0.5, 0.1875, ((0, 32),)),
        "list0": draw_list0(jax.random.fold_in(splits[20], 71), 0),
        "list1": draw_list1(jax.random.fold_in(splits[20], 71), 0),
        "list2": draw_list2(jax.random.fold_in(splits[20], 71), 0),
        "mask0": draw_mask0(jax.random.fold_in(splits[20], 71), 0),
        "mask1": draw_mask1(jax.random.fold_in(splits[20], 71), 0),
        "mask2": draw_mask2(jax.random.fold_in(splits[20], 71), 0),
        "top_list": plant(jax.random.randint(splits[15], (TOPS, KT), 0, TOPS), jax.random.fold_in(splits[15], 1), 0, TOPS - 1).astype(jnp.int32),
        "top_mask": plant((jax.random.randint(splits[16], (TOPS, KT), 0, 4) < 3).astype(jnp.int32), jax.random.fold_in(splits[16], 1), 0, 1),
        "near_tiles": scatter_about(splits[17], (LEAVES, NEAR, LEAF, LEAF), (LEAF * NEAR) ** -0.5, 0.1875, ((0, 32),)),
        "near_list": draw_near_list(jax.random.fold_in(splits[20], 71), 0),
        "near_mask": draw_near_mask(jax.random.fold_in(splits[20], 71), 0),
    }


def lift(coef, transfer):
    part = jnp.einsum("crq,cnr->cnq", transfer.astype(jnp.float32), coef.astype(jnp.float32))
    part = part.reshape(part.shape[0] // 2, 2, part.shape[1], part.shape[2])
    return part.sum(axis=1).astype(jnp.bfloat16)


def lower(field, transfer, parent):
    spread = jnp.repeat(parent, 2, axis=0)
    total = field + jnp.einsum("crq,cnq->cnr", transfer.astype(jnp.float32), spread.astype(jnp.float32))
    return total.astype(jnp.bfloat16)


def group_offset(links, count):
    rows = links.shape[0]
    base = (jnp.arange(rows, dtype=jnp.int32) // (N_LEAF * count)) * (N_LEAF * count)
    return (links + base[:, None]).astype(jnp.int32)


def couple(table, source, links, valid):
    blocks = N_BRANCH * N_LEAF

    def one(item):
        tab, idx, live = item
        picked = source[idx].astype(jnp.float32) * live[:, :, None, None].astype(jnp.float32)
        return jnp.einsum("ckrs,ckns->cnr", tab.astype(jnp.float32), picked)

    out = lax.map(one, (table.reshape((blocks, -1) + table.shape[1:]),
                        links.reshape(blocks, -1, links.shape[1]),
                        valid.reshape(blocks, -1, valid.shape[1])))
    return out.reshape((-1,) + out.shape[2:])


def reference(charges, basis, transfer0, transfer1, transfer2, couple0, couple1, couple2, couple_top,
              list0, list1, list2, mask0, mask1, mask2, top_list, top_mask, near_tiles, near_list, near_mask):
    coef = jnp.einsum("lpr,lnp->lnr", basis.astype(jnp.float32), charges.astype(jnp.float32)).astype(jnp.bfloat16)
    transfers = (transfer0, transfer1, transfer2)
    levels = [coef]
    for table in transfers:
        coef = lift(coef, table)
        levels.append(coef)
    fields = []
    for level, table, links, valid in zip(levels[:3], (couple0, couple1, couple2), (list0, list1, list2), (mask0, mask1, mask2)):
        count = level.shape[0] // (N_BRANCH * N_LEAF)
        fields.append(couple(table, level, group_offset(links, count), valid))
    field_top = couple(couple_top, levels[3], top_list, top_mask)
    local = field_top.astype(jnp.bfloat16)
    for step in (2, 1, 0):
        local = lower(fields[step], transfers[step], local)
    near = couple(near_tiles, charges, group_offset(near_list, CL_DEV), near_mask)
    return jnp.einsum("lpr,lnr->lnp", basis.astype(jnp.float32), local.astype(jnp.float32)) + near
```

```python
import functools

import jax
import jax.numpy as jnp
from jax import lax
from jax.experimental import pallas as pl
from jax.experimental.pallas import tpu as pltpu
from jax.sharding import PartitionSpec as P

MESH = pl.DeviceIdType.MESH
BF = jnp.bfloat16
F32 = jnp.float32


def nn(a, b):
    return lax.dot_general(a, b, (((1,), (0,)), ((), ())), preferred_element_type=F32)


def nt(a, b):
    return lax.dot_general(a, b, (((1,), (1,)), ((), ())), preferred_element_type=F32)


def gathered(table, c, wide, start, spot):
    total = None
    width = table.shape[1]
    for k in range(0, width, 2):
        left = jnp.concatenate([wide[spot(k)], wide[spot(k + 1)]], axis=1)
        right = jnp.concatenate([table[c, k], table[c, k + 1]], axis=1)
        part = nt(left, right)
        total = part if total is None else total + part
    return total


def kernel(
    n_branch,
    n_leaf,
    charges,
    basis,
    transfer0,
    transfer1,
    transfer2,
    couple0,
    couple1,
    couple2,
    couple_top,
    list0,
    list1,
    list2,
    mask0,
    mask1,
    mask2,
    top_list,
    top_mask,
    near_tiles,
    near_list,
    near_mask,
    out,
    v_basis,
    v_t0,
    v_t1,
    v_t2,
    v_c0,
    v_c1,
    v_c2,
    v_ct,
    v_near,
    s_l0,
    s_l1,
    s_l2,
    s_m0,
    s_m1,
    s_m2,
    s_tl,
    s_tm,
    s_nl,
    s_nm,
    w_ch,
    w_co,
    w_top,
    load_sem,
    list_sem,
    send_sem,
    recv_sem,
    top_send,
    top_recv,
):
    branch = lax.axis_index("branch")
    leaf = lax.axis_index("leaf")
    total = n_branch * n_leaf
    me = branch * n_leaf + leaf
    n0 = basis.shape[0]
    n1, n2 = n0 // 2, n0 // 4
    own = n0 + n1 + n2

    def target(i):
        t = lax.rem(me + i, total)
        return {"branch": t // n_leaf, "leaf": lax.rem(t, n_leaf)}

    loads = {}
    pairs = [
        ("ch", charges, w_ch.at[pl.ds(n0, n0)]),
        ("basis", basis, v_basis),
        ("t0", transfer0, v_t0),
        ("t1", transfer1, v_t1),
        ("t2", transfer2, v_t2),
        ("near", near_tiles, v_near),
        ("c0", couple0, v_c0),
        ("c1", couple1, v_c1),
        ("c2", couple2, v_c2),
        ("ct", couple_top, v_ct),
    ]
    for i, (name, src, dst) in enumerate(pairs):
        loads[name] = pltpu.make_async_copy(src, dst, load_sem.at[i])
    lists = []
    for i, (src, dst) in enumerate(
        [
            (near_list, s_nl),
            (near_mask, s_nm),
            (list0, s_l0),
            (mask0, s_m0),
            (list1, s_l1),
            (mask1, s_m1),
            (list2, s_l2),
            (mask2, s_m2),
            (top_list, s_tl),
            (top_mask, s_tm),
        ]
    ):
        lists.append(pltpu.make_async_copy(src, dst, list_sem.at[i]))
    for name in ("ch", "basis", "t0", "t1", "t2"):
        loads[name].start()

    barrier = pltpu.get_barrier_semaphore()

    @pl.loop(1, total)
    def _(i):
        pl.semaphore_signal(barrier, inc=1, device_id=target(i), device_id_type=MESH)

    for item in lists:
        item.start()
    for name in ("near", "c0", "c1", "c2", "ct"):
        loads[name].start()

    blank = jnp.zeros(w_ch.shape[1:], BF)
    w_ch[3 * n0] = blank
    w_co[3 * own] = blank
    w_top[total] = blank

    loads["ch"].wait()
    loads["basis"].wait()
    for c in range(n0):
        w_co[own + c] = nn(w_ch[n0 + c], v_basis[c]).astype(BF)

    pl.semaphore_wait(barrier, total - 1)

    def hop(buf, size, slot, step, dst_row):
        return pltpu.make_async_remote_copy(
            src_ref=buf.at[pl.ds(size, size)],
            dst_ref=buf.at[pl.ds(dst_row, size)],
            send_sem=send_sem.at[slot],
            recv_sem=recv_sem.at[slot],
            device_id={"branch": branch, "leaf": leaf + step},
            device_id_type=MESH,
        )

    ch_right = hop(w_ch, n0, 0, 1, 0)
    ch_left = hop(w_ch, n0, 1, -1, 2 * n0)
    co_right = hop(w_co, own, 2, 1, 0)
    co_left = hop(w_co, own, 3, -1, 2 * own)
    has_left = leaf > 0
    has_right = leaf < n_leaf - 1

    @pl.when(has_right)
    def _():
        ch_right.start()

    @pl.when(has_left)
    def _():
        ch_left.start()

    loads["t0"].wait()
    loads["t1"].wait()
    loads["t2"].wait()
    at = own
    for table, count in ((v_t0, n1), (v_t1, n2), (v_t2, n2 // 2)):
        for p in range(count):
            left = jnp.concatenate([w_co[at + 2 * p], w_co[at + 2 * p + 1]], axis=1)
            right = jnp.concatenate([table[2 * p], table[2 * p + 1]], axis=0)
            value = nn(left, right).astype(BF)
            if table is v_t2:
                w_top[me] = value
            else:
                w_co[at + 2 * count + p] = value
        at = at + 2 * count

    @pl.when(has_right)
    def _():
        co_right.start()

    @pl.when(has_left)
    def _():
        co_left.start()

    @pl.loop(1, total)
    def _(i):
        pltpu.make_async_remote_copy(
            src_ref=w_top.at[me],
            dst_ref=w_top.at[me],
            send_sem=top_send,
            recv_sem=top_recv,
            device_id=target(i),
            device_id_type=MESH,
        ).start()

    for item in lists:
        item.wait()
    loads["near"].wait()

    @pl.when(has_left)
    def _():
        ch_right.wait_recv()

    @pl.when(has_right)
    def _():
        ch_left.wait_recv()

    def where_of(links, valid, c, shift, blank_row):
        return lambda k: jnp.where(valid[c, k] != 0, links[c, k] - shift, blank_row)

    for c in range(n0):
        spot = where_of(s_nl, s_nm, c, (leaf - 1) * n0, 3 * n0)
        out[c] = gathered(v_near, c, w_ch, 0, spot)

    @pl.when(has_left)
    def _():
        co_right.wait_recv()

    @pl.when(has_right)
    def _():
        co_left.wait_recv()

    loads["c0"].wait()
    loads["c1"].wait()
    loads["c2"].wait()
    loads["ct"].wait()

    def level_spot(links, valid, c, count, start):
        def spot(k):
            j = links[c, k] - (leaf - 1) * count
            side = j // count
            row = side * own + (j - side * count) + start
            return jnp.where(valid[c, k] != 0, row, 3 * own)

        return spot

    fields = []
    for table, links, valid, count, start in (
        (v_c0, s_l0, s_m0, n0, 0),
        (v_c1, s_l1, s_m1, n1, n0),
        (v_c2, s_l2, s_m2, n2, n0 + n1),
    ):
        fields.append(
            [gathered(table, c, w_co, 0, level_spot(links, valid, c, count, start)) for c in range(count)]
        )

    everyone = w_top.at[pl.ds(0, total - 1)]
    pltpu.make_async_copy(everyone, everyone, top_recv).wait()
    local = [
        gathered(v_ct, c, w_top, 0, where_of(s_tl, s_tm, c, 0, total)).astype(BF)
        for c in range(couple_top.shape[0])
    ]
    for field, table in ((fields[2], v_t2), (fields[1], v_t1), (fields[0], v_t0)):
        below = []
        for p, parent in enumerate(local):
            both = jnp.concatenate([table[2 * p], table[2 * p + 1]], axis=0)
            spread = nt(parent, both)
            width = table.shape[1]
            below.append((field[2 * p] + spread[:, :width]).astype(BF))
            below.append((field[2 * p + 1] + spread[:, width:]).astype(BF))
        local = below
    for c in range(n0):
        out[c] += nt(local[c], v_basis[c])

    @pl.when(has_right)
    def _():
        ch_right.wait_send()
        co_right.wait_send()

    @pl.when(has_left)
    def _():
        ch_left.wait_send()
        co_left.wait_send()

    pltpu.make_async_copy(everyone, everyone, top_send).wait()


def solution(mesh):
    n_branch, n_leaf = mesh.shape["branch"], mesh.shape["leaf"]
    total = n_branch * n_leaf

    def per_device(*args):
        (charges, basis, t0, t1, t2, c0, c1, c2, ct, l0, l1, l2, m0, m1, m2, tl, tm, near, nl, nm) = args
        n0 = charges.shape[0]
        tile = charges.shape[1:]
        own = n0 + n0 // 2 + n0 // 4
        vmem = lambda x: pltpu.VMEM(x.shape, x.dtype)
        smem = lambda x: pltpu.SMEM(x.shape, x.dtype)
        dma = pltpu.SemaphoreType.DMA
        return pl.pallas_call(
            functools.partial(kernel, n_branch, n_leaf),
            out_shape=jax.ShapeDtypeStruct(charges.shape, F32),
            in_specs=[pl.BlockSpec(memory_space=pl.ANY)] * len(args),
            out_specs=pl.BlockSpec(memory_space=pltpu.VMEM),
            scratch_shapes=[
                *[vmem(x) for x in (basis, t0, t1, t2, c0, c1, c2, ct, near)],
                *[smem(x) for x in (l0, l1, l2, m0, m1, m2, tl, tm, nl, nm)],
                pltpu.VMEM((3 * n0 + 1, *tile), BF),
                pltpu.VMEM((3 * own + 1, *tile), BF),
                pltpu.VMEM((total + 1, *tile), BF),
                dma((10,)),
                dma((10,)),
                dma((4,)),
                dma((4,)),
                dma(()),
                dma(()),
            ],
            compiler_params=pltpu.CompilerParams(
                collective_id=0, has_side_effects=True, vmem_limit_bytes=40 * 1024 * 1024
            ),
        )(*args)

    three, four, two = P(("branch", "leaf"), None, None), P(("branch", "leaf"), None, None, None), P(("branch", "leaf"), None)
    return jax.shard_map(
        per_device,
        mesh=mesh,
        in_specs=(*[three] * 5, *[four] * 4, *[two] * 8, four, two, two),
        out_specs=three,
        check_vma=False,
    )
```

```python
import functools

import jax
import jax.numpy as jnp
from jax import lax
from jax.experimental import pallas as pl
from jax.experimental.pallas import tpu as pltpu
from jax.sharding import PartitionSpec as P

MESH = pl.DeviceIdType.MESH
BF = jnp.bfloat16
F32 = jnp.float32


def nn(a, b):
    return lax.dot_general(a, b, (((1,), (0,)), ((), ())), preferred_element_type=F32)


def nt(a, b):
    return lax.dot_general(a, b, (((1,), (1,)), ((), ())), preferred_element_type=F32)


def gathered(table, c, wide, start, spot):
    total = None
    width = table.shape[1]
    for k in range(0, width, 2):
        left = jnp.concatenate([wide[spot(k)], wide[spot(k + 1)]], axis=1)
        right = jnp.concatenate([table[c, k], table[c, k + 1]], axis=1)
        part = nt(left, right)
        total = part if total is None else total + part
    return total


def kernel(
    n_branch,
    n_leaf,
    charges,
    basis,
    transfer0,
    transfer1,
    transfer2,
    couple0,
    couple1,
    couple2,
    couple_top,
    list0,
    list1,
    list2,
    mask0,
    mask1,
    mask2,
    top_list,
    top_mask,
    near_tiles,
    near_list,
    near_mask,
    out,
    v_basis,
    v_t0,
    v_t1,
    v_t2,
    v_c0,
    v_c1,
    v_c2,
    v_ct,
    v_near,
    s_l0,
    s_l1,
    s_l2,
    s_m0,
    s_m1,
    s_m2,
    s_tl,
    s_tm,
    s_nl,
    s_nm,
    w_ch,
    w_co,
    w_top,
    load_sem,
    list_sem,
    send_sem,
    recv_sem,
    top_send,
    top_recv,
):
    branch = lax.axis_index("branch")
    leaf = lax.axis_index("leaf")
    total = n_branch * n_leaf
    me = branch * n_leaf + leaf
    n0 = basis.shape[0]
    n1, n2 = n0 // 2, n0 // 4
    own = n0 + n1 + n2

    def around(place, step, count):
        there = place + step
        return jnp.where(there >= count, there - count, there)

    def each_device(act):
        for db in range(n_branch):
            there = around(branch, db, n_branch)
            first = 1 if db == 0 else 0
            if n_leaf <= 8:
                for dl in range(first, n_leaf):
                    act({"branch": there, "leaf": around(leaf, dl, n_leaf)})
            else:

                @pl.loop(first, n_leaf)
                def _(dl):
                    act({"branch": there, "leaf": around(leaf, dl, n_leaf)})

    loads = {}
    pairs = [
        ("ch", charges, w_ch.at[pl.ds(n0, n0)]),
        ("basis", basis, v_basis),
        ("t0", transfer0, v_t0),
        ("t1", transfer1, v_t1),
        ("t2", transfer2, v_t2),
        ("near", near_tiles, v_near),
        ("c0", couple0, v_c0),
        ("c1", couple1, v_c1),
        ("c2", couple2, v_c2),
        ("ct", couple_top, v_ct),
    ]
    for i, (name, src, dst) in enumerate(pairs):
        loads[name] = pltpu.make_async_copy(src, dst, load_sem.at[i])
    lists = []
    for i, (src, dst) in enumerate(
        [
            (near_list, s_nl),
            (near_mask, s_nm),
            (list0, s_l0),
            (mask0, s_m0),
            (list1, s_l1),
            (mask1, s_m1),
            (list2, s_l2),
            (mask2, s_m2),
            (top_list, s_tl),
            (top_mask, s_tm),
        ]
    ):
        lists.append(pltpu.make_async_copy(src, dst, list_sem.at[i]))
    for name in ("ch", "basis", "t0", "t1", "t2"):
        loads[name].start()

    barrier = pltpu.get_barrier_semaphore()

    each_device(
        lambda there: pl.semaphore_signal(barrier, inc=1, device_id=there, device_id_type=MESH)
    )

    for item in lists:
        item.start()
    for name in ("near", "c0", "c1", "c2", "ct"):
        loads[name].start()

    blank = jnp.zeros(w_ch.shape[1:], BF)
    w_ch[3 * n0] = blank
    w_co[3 * own] = blank
    w_top[total] = blank

    loads["ch"].wait()
    loads["basis"].wait()
    for c in range(n0):
        w_co[own + c] = nn(w_ch[n0 + c], v_basis[c]).astype(BF)

    def hop(buf, size, slot, step, dst_row):
        return pltpu.make_async_remote_copy(
            src_ref=buf.at[pl.ds(size, size)],
            dst_ref=buf.at[pl.ds(dst_row, size)],
            send_sem=send_sem.at[slot],
            recv_sem=recv_sem.at[slot],
            device_id={"branch": branch, "leaf": leaf + step},
            device_id_type=MESH,
        )

    ch_right = hop(w_ch, n0, 0, 1, 0)
    ch_left = hop(w_ch, n0, 1, -1, 2 * n0)
    co_right = hop(w_co, own, 2, 1, 0)
    co_left = hop(w_co, own, 3, -1, 2 * own)
    has_left = leaf > 0
    has_right = leaf < n_leaf - 1

    loads["t0"].wait()
    loads["t1"].wait()
    loads["t2"].wait()
    at = own
    for table, count in ((v_t0, n1), (v_t1, n2), (v_t2, n2 // 2)):
        for p in range(count):
            left = jnp.concatenate([w_co[at + 2 * p], w_co[at + 2 * p + 1]], axis=1)
            right = jnp.concatenate([table[2 * p], table[2 * p + 1]], axis=0)
            value = nn(left, right).astype(BF)
            if table is v_t2:
                w_top[me] = value
            else:
                w_co[at + 2 * count + p] = value
        at = at + 2 * count

    pl.semaphore_wait(barrier, total - 1)
    each_device(
        lambda there: pltpu.make_async_remote_copy(
            src_ref=w_top.at[me],
            dst_ref=w_top.at[me],
            send_sem=top_send,
            recv_sem=top_recv,
            device_id=there,
            device_id_type=MESH,
        ).start()
    )

    @pl.when(has_right)
    def _():
        ch_right.start()

    @pl.when(has_left)
    def _():
        ch_left.start()

    @pl.when(has_right)
    def _():
        co_right.start()

    @pl.when(has_left)
    def _():
        co_left.start()

    for item in lists:
        item.wait()
    loads["near"].wait()

    @pl.when(has_left)
    def _():
        ch_right.wait_recv()

    @pl.when(has_right)
    def _():
        ch_left.wait_recv()

    def where_of(links, valid, c, shift, blank_row):
        return lambda k: jnp.where(valid[c, k] != 0, links[c, k] - shift, blank_row)

    for c in range(n0):
        spot = where_of(s_nl, s_nm, c, (leaf - 1) * n0, 3 * n0)
        out[c] = gathered(v_near, c, w_ch, 0, spot)

    @pl.when(has_left)
    def _():
        co_right.wait_recv()

    @pl.when(has_right)
    def _():
        co_left.wait_recv()

    loads["c0"].wait()
    loads["c1"].wait()
    loads["c2"].wait()
    loads["ct"].wait()

    def level_spot(links, valid, c, count, start):
        def spot(k):
            j = links[c, k] - (leaf - 1) * count
            side = j // count
            row = side * own + (j - side * count) + start
            return jnp.where(valid[c, k] != 0, row, 3 * own)

        return spot

    fields = []
    for table, links, valid, count, start in (
        (v_c0, s_l0, s_m0, n0, 0),
        (v_c1, s_l1, s_m1, n1, n0),
        (v_c2, s_l2, s_m2, n2, n0 + n1),
    ):
        fields.append(
            [gathered(table, c, w_co, 0, level_spot(links, valid, c, count, start)) for c in range(count)]
        )

    everyone = w_top.at[pl.ds(0, total - 1)]
    pltpu.make_async_copy(everyone, everyone, top_recv).wait()
    local = [
        gathered(v_ct, c, w_top, 0, where_of(s_tl, s_tm, c, 0, total)).astype(BF)
        for c in range(couple_top.shape[0])
    ]
    for field, table in ((fields[2], v_t2), (fields[1], v_t1), (fields[0], v_t0)):
        below = []
        for p, parent in enumerate(local):
            both = jnp.concatenate([table[2 * p], table[2 * p + 1]], axis=0)
            spread = nt(parent, both)
            width = table.shape[1]
            below.append((field[2 * p] + spread[:, :width]).astype(BF))
            below.append((field[2 * p + 1] + spread[:, width:]).astype(BF))
        local = below
    for c in range(n0):
        out[c] += nt(local[c], v_basis[c])

    @pl.when(has_right)
    def _():
        ch_right.wait_send()
        co_right.wait_send()

    @pl.when(has_left)
    def _():
        ch_left.wait_send()
        co_left.wait_send()

    pltpu.make_async_copy(everyone, everyone, top_send).wait()


def solution(mesh):
    n_branch, n_leaf = mesh.shape["branch"], mesh.shape["leaf"]
    total = n_branch * n_leaf

    def per_device(*args):
        (charges, basis, t0, t1, t2, c0, c1, c2, ct, l0, l1, l2, m0, m1, m2, tl, tm, near, nl, nm) = args
        n0 = charges.shape[0]
        tile = charges.shape[1:]
        own = n0 + n0 // 2 + n0 // 4
        vmem = lambda x: pltpu.VMEM(x.shape, x.dtype)
        smem = lambda x: pltpu.SMEM(x.shape, x.dtype)
        dma = pltpu.SemaphoreType.DMA
        return pl.pallas_call(
            functools.partial(kernel, n_branch, n_leaf),
            out_shape=jax.ShapeDtypeStruct(charges.shape, F32),
            in_specs=[pl.BlockSpec(memory_space=pl.ANY)] * len(args),
            out_specs=pl.BlockSpec(memory_space=pltpu.VMEM),
            scratch_shapes=[
                *[vmem(x) for x in (basis, t0, t1, t2, c0, c1, c2, ct, near)],
                *[smem(x) for x in (l0, l1, l2, m0, m1, m2, tl, tm, nl, nm)],
                pltpu.VMEM((3 * n0 + 1, *tile), BF),
                pltpu.VMEM((3 * own + 1, *tile), BF),
                pltpu.VMEM((total + 1, *tile), BF),
                dma((10,)),
                dma((10,)),
                dma((4,)),
                dma((4,)),
                dma(()),
                dma(()),
            ],
            compiler_params=pltpu.CompilerParams(
                collective_id=0, has_side_effects=True, vmem_limit_bytes=63 * 1024 * 1024
            ),
        )(*args)

    three, four, two = P(("branch", "leaf"), None, None), P(("branch", "leaf"), None, None, None), P(("branch", "leaf"), None)
    return jax.shard_map(
        per_device,
        mesh=mesh,
        in_specs=(*[three] * 5, *[four] * 4, *[two] * 8, four, two, two),
        out_specs=three,
        check_vma=False,
    )
```

```python
import functools

import jax
import jax.numpy as jnp
from jax import lax
from jax.experimental import pallas as pl
from jax.experimental.pallas import tpu as pltpu
from jax.sharding import PartitionSpec as P

MESH = pl.DeviceIdType.MESH
BF = jnp.bfloat16
F32 = jnp.float32


def nn(a, b):
    return lax.dot_general(a, b, (((1,), (0,)), ((), ())), preferred_element_type=F32)


def nt(a, b):
    return lax.dot_general(a, b, (((1,), (1,)), ((), ())), preferred_element_type=F32)


def gathered(table, c, wide, start, spot):
    total = None
    width = table.shape[1]
    for k in range(0, width, 2):
        left = jnp.concatenate([wide[spot(k)], wide[spot(k + 1)]], axis=1)
        right = jnp.concatenate([table[c, k], table[c, k + 1]], axis=1)
        part = nt(left, right)
        total = part if total is None else total + part
    return total


def kernel(
    n_branch,
    n_leaf,
    charges,
    basis,
    transfer0,
    transfer1,
    transfer2,
    couple0,
    couple1,
    couple2,
    couple_top,
    list0,
    list1,
    list2,
    mask0,
    mask1,
    mask2,
    top_list,
    top_mask,
    near_tiles,
    near_list,
    near_mask,
    result,
    v_basis,
    v_t0,
    v_t1,
    v_t2,
    v_c0,
    v_c1,
    v_c2,
    v_ct,
    v_near,
    s_l0,
    s_l1,
    s_l2,
    s_m0,
    s_m1,
    s_m2,
    s_tl,
    s_tm,
    s_nl,
    s_nm,
    w_ch,
    w_co,
    w_top,
    out,
    out_sem,
    load_sem,
    list_sem,
    send_sem,
    recv_sem,
    top_send,
    top_recv,
):
    branch = lax.axis_index("branch")
    leaf = lax.axis_index("leaf")
    total = n_branch * n_leaf
    me = branch * n_leaf + leaf
    n0 = basis.shape[0]
    n1, n2 = n0 // 2, n0 // 4
    own = n0 + n1 + n2

    def around(place, step, count):
        there = place + step
        return jnp.where(there >= count, there - count, there)

    def each_device(act):
        for db in range(n_branch):
            there = around(branch, db, n_branch)
            first = 1 if db == 0 else 0
            if n_leaf <= 8:
                for dl in range(first, n_leaf):
                    act({"branch": there, "leaf": around(leaf, dl, n_leaf)})
            else:

                @pl.loop(first, n_leaf)
                def _(dl):
                    act({"branch": there, "leaf": around(leaf, dl, n_leaf)})

    loads = {}
    pairs = [
        ("ch", charges, w_ch.at[pl.ds(n0, n0)]),
        ("basis", basis, v_basis),
        ("t0", transfer0, v_t0),
        ("t1", transfer1, v_t1),
        ("t2", transfer2, v_t2),
        ("near", near_tiles, v_near),
        ("c0", couple0, v_c0),
        ("c1", couple1, v_c1),
        ("c2", couple2, v_c2),
        ("ct", couple_top, v_ct),
    ]
    for i, (name, src, dst) in enumerate(pairs):
        loads[name] = pltpu.make_async_copy(src, dst, load_sem.at[i])
    lists = []
    for i, (src, dst) in enumerate(
        [
            (near_list, s_nl),
            (near_mask, s_nm),
            (list0, s_l0),
            (mask0, s_m0),
            (list1, s_l1),
            (mask1, s_m1),
            (list2, s_l2),
            (mask2, s_m2),
            (top_list, s_tl),
            (top_mask, s_tm),
        ]
    ):
        lists.append(pltpu.make_async_copy(src, dst, list_sem.at[i]))
    for name in ("ch", "basis", "t0", "t1", "t2"):
        loads[name].start()

    barrier = pltpu.get_barrier_semaphore()

    each_device(
        lambda there: pl.semaphore_signal(barrier, inc=1, device_id=there, device_id_type=MESH)
    )

    for item in lists:
        item.start()
    for name in ("near", "c0", "c1", "c2", "ct"):
        loads[name].start()

    blank = jnp.zeros(w_ch.shape[1:], BF)
    w_ch[3 * n0] = blank
    w_co[3 * own] = blank
    w_top[total] = blank

    loads["ch"].wait()
    loads["basis"].wait()
    for c in range(n0):
        w_co[own + c] = nn(w_ch[n0 + c], v_basis[c]).astype(BF)

    def hop(buf, size, slot, step, dst_row):
        return pltpu.make_async_remote_copy(
            src_ref=buf.at[pl.ds(size, size)],
            dst_ref=buf.at[pl.ds(dst_row, size)],
            send_sem=send_sem.at[slot],
            recv_sem=recv_sem.at[slot],
            device_id={"branch": branch, "leaf": leaf + step},
            device_id_type=MESH,
        )

    ch_right = hop(w_ch, n0, 0, 1, 0)
    ch_left = hop(w_ch, n0, 1, -1, 2 * n0)
    co_right = hop(w_co, own, 2, 1, 0)
    co_left = hop(w_co, own, 3, -1, 2 * own)
    has_left = leaf > 0
    has_right = leaf < n_leaf - 1

    loads["t0"].wait()
    loads["t1"].wait()
    loads["t2"].wait()
    at = own
    for table, count in ((v_t0, n1), (v_t1, n2), (v_t2, n2 // 2)):
        for p in range(count):
            left = jnp.concatenate([w_co[at + 2 * p], w_co[at + 2 * p + 1]], axis=1)
            right = jnp.concatenate([table[2 * p], table[2 * p + 1]], axis=0)
            value = nn(left, right).astype(BF)
            if table is v_t2:
                w_top[me] = value
            else:
                w_co[at + 2 * count + p] = value
        at = at + 2 * count

    pl.semaphore_wait(barrier, total - 1)
    each_device(
        lambda there: pltpu.make_async_remote_copy(
            src_ref=w_top.at[me],
            dst_ref=w_top.at[me],
            send_sem=top_send,
            recv_sem=top_recv,
            device_id=there,
            device_id_type=MESH,
        ).start()
    )

    @pl.when(has_right)
    def _():
        ch_right.start()

    @pl.when(has_left)
    def _():
        ch_left.start()

    @pl.when(has_right)
    def _():
        co_right.start()

    @pl.when(has_left)
    def _():
        co_left.start()

    for item in lists:
        item.wait()
    loads["near"].wait()

    @pl.when(has_left)
    def _():
        ch_right.wait_recv()

    @pl.when(has_right)
    def _():
        ch_left.wait_recv()

    def where_of(links, valid, c, shift, blank_row):
        return lambda k: jnp.where(valid[c, k] != 0, links[c, k] - shift, blank_row)

    for c in range(n0):
        spot = where_of(s_nl, s_nm, c, (leaf - 1) * n0, 3 * n0)
        out[c] = gathered(v_near, c, w_ch, 0, spot)

    @pl.when(has_left)
    def _():
        co_right.wait_recv()

    @pl.when(has_right)
    def _():
        co_left.wait_recv()

    loads["c0"].wait()
    loads["c1"].wait()
    loads["c2"].wait()
    loads["ct"].wait()

    def level_spot(links, valid, c, count, start):
        def spot(k):
            j = links[c, k] - (leaf - 1) * count
            side = j // count
            row = side * own + (j - side * count) + start
            return jnp.where(valid[c, k] != 0, row, 3 * own)

        return spot

    fields = []
    for table, links, valid, count, start in (
        (v_c0, s_l0, s_m0, n0, 0),
        (v_c1, s_l1, s_m1, n1, n0),
        (v_c2, s_l2, s_m2, n2, n0 + n1),
    ):
        fields.append(
            [gathered(table, c, w_co, 0, level_spot(links, valid, c, count, start)) for c in range(count)]
        )

    everyone = w_top.at[pl.ds(0, total - 1)]
    pltpu.make_async_copy(everyone, everyone, top_recv).wait()
    local = [
        gathered(v_ct, c, w_top, 0, where_of(s_tl, s_tm, c, 0, total)).astype(BF)
        for c in range(couple_top.shape[0])
    ]
    for field, table in ((fields[2], v_t2), (fields[1], v_t1), (fields[0], v_t0)):
        below = []
        for p, parent in enumerate(local):
            both = jnp.concatenate([table[2 * p], table[2 * p + 1]], axis=0)
            spread = nt(parent, both)
            width = table.shape[1]
            below.append((field[2 * p] + spread[:, :width]).astype(BF))
            below.append((field[2 * p + 1] + spread[:, width:]).astype(BF))
        local = below
    for c in range(n0):
        out[c] += nt(local[c], v_basis[c])
        pltpu.make_async_copy(out.at[c], result.at[c], out_sem.at[c]).start()

    @pl.when(has_right)
    def _():
        ch_right.wait_send()
        co_right.wait_send()

    @pl.when(has_left)
    def _():
        ch_left.wait_send()
        co_left.wait_send()

    pltpu.make_async_copy(everyone, everyone, top_send).wait()
    for c in range(n0):
        pltpu.make_async_copy(out.at[c], result.at[c], out_sem.at[c]).wait()


def solution(mesh):
    n_branch, n_leaf = mesh.shape["branch"], mesh.shape["leaf"]
    total = n_branch * n_leaf

    def per_device(*args):
        (charges, basis, t0, t1, t2, c0, c1, c2, ct, l0, l1, l2, m0, m1, m2, tl, tm, near, nl, nm) = args
        n0 = charges.shape[0]
        tile = charges.shape[1:]
        own = n0 + n0 // 2 + n0 // 4
        vmem = lambda x: pltpu.VMEM(x.shape, x.dtype)
        smem = lambda x: pltpu.SMEM(x.shape, x.dtype)
        dma = pltpu.SemaphoreType.DMA
        return pl.pallas_call(
            functools.partial(kernel, n_branch, n_leaf),
            out_shape=jax.ShapeDtypeStruct(charges.shape, F32),
            in_specs=[pl.BlockSpec(memory_space=pl.ANY)] * len(args),
            out_specs=pl.BlockSpec(memory_space=pl.ANY),
            scratch_shapes=[
                *[vmem(x) for x in (basis, t0, t1, t2, c0, c1, c2, ct, near)],
                *[smem(x) for x in (l0, l1, l2, m0, m1, m2, tl, tm, nl, nm)],
                pltpu.VMEM((3 * n0 + 1, *tile), BF),
                pltpu.VMEM((3 * own + 1, *tile), BF),
                pltpu.VMEM((total + 1, *tile), BF),
                pltpu.VMEM(charges.shape, F32),
                dma((n0,)),
                dma((10,)),
                dma((10,)),
                dma((4,)),
                dma((4,)),
                dma(()),
                dma(()),
            ],
            compiler_params=pltpu.CompilerParams(
                collective_id=0, has_side_effects=True, vmem_limit_bytes=63 * 1024 * 1024
            ),
        )(*args)

    three, four, two = P(("branch", "leaf"), None, None), P(("branch", "leaf"), None, None, None), P(("branch", "leaf"), None)
    return jax.shard_map(
        per_device,
        mesh=mesh,
        in_specs=(*[three] * 5, *[four] * 4, *[two] * 8, four, two, two),
        out_specs=three,
        check_vma=False,
    )
```
